32 devices in a mesh: dp: 4 (over x, core), grid: 8 (over z, y).
Axes of the slice: x: 2, y: 2, z: 4, core: 2. Of those that a mesh axis runs over, the one named last changes fastest.
Arguments:
- q_row: bfloat16 [8, 96, 96, 1536], P('dp', 'grid'), may hold values from -8 to 8, as said below
- k_row: bfloat16 [8, 96, 96, 1536], P('dp', 'grid'), may hold values from -8 to 8
- v_row: bfloat16 [8, 96, 96, 1536], P('dp', 'grid'), may hold values from -6 to 6
- q_col: bfloat16 [8, 96, 96, 1536], P('dp', None, 'grid'), may hold values from -8 to 8, as said below
- k_col: bfloat16 [8, 96, 96, 1536], P('dp', None, 'grid'), may hold values from -8 to 8
- cotangent: bfloat16 [8, 96, 96, 1536], P('dp', None, 'grid'), may hold values from -6 to 6
- w_value: bfloat16 [1536, 1536], P(('dp', 'grid')), may hold values from -0.15625 to 0.15625
- row_positions: int32 [96], replicated, may hold values from 0 to 95, each once
- col_positions: int32 [96], replicated, may hold values from 0 to 95, each once
- mlp_in: float32 [512], P('grid'), may hold values from -8 to 8
- mlp_bias: float32 [512], P('grid'), may hold values from -4 to 4
- mlp_out: float32 [512, 48], P('grid'), may hold values from -0.08 to 0.08
Outputs:
- attended: bfloat16 [8, 96, 96, 1536], P('dp', None, 'grid')
- grad_mlp_in: float32 [512], P('grid')
- grad_mlp_bias: float32 [512], P('grid')
- grad_mlp_out: float32 [512, 48], P('grid')
The draws below stay inside these ranges and needn't reach their ends.
Inputs may be any that keep to these rules, and one draw needn't show every extreme that they name: q_row and k_row lie within the range. q_col and k_col lie within the range. `row_positions`: each of 0 to 95 appears once. `col_positions`: each of 0 to 95 appears once.
All inputs are finite; a program needn't handle non-finite values.
Results may differ from the reference program's by a relative error of at most 0.007.
Values may be sent and summed in bfloat16 or wider, within the bound.
A program may use at most 384 MiB of HBM per device.

```python
import jax
import jax.numpy as jnp
from jax import lax

G = 96
D = 1536
NH = 48
HD = 32
HM = 512
NOFF = 191
BATCH = 8


def draw_attention_pair(key):
    shape = (BATCH, G, G, D)
    key_out = jnp.clip(jax.random.normal(jax.random.fold_in(key, 31), shape, jnp.float32), -6.0, 6.0)
    query_out = jnp.clip(jax.random.normal(jax.random.fold_in(key, 32), shape, jnp.float32), -6.0, 6.0)
    return (query_out, key_out)


def draw_q_row(key, part):
    return draw_attention_pair(jax.random.fold_in(key, 1))[0].astype(jnp.bfloat16)


def draw_k_row(key, part):
    return draw_attention_pair(jax.random.fold_in(key, 1))[1].astype(jnp.bfloat16)


def draw_q_col(key, part):
    return draw_attention_pair(jax.random.fold_in(key, 2))[0].astype(jnp.bfloat16)


def draw_k_col(key, part):
    return draw_attention_pair(jax.random.fold_in(key, 2))[1].astype(jnp.bfloat16)


def block_scale(own_key, dims, split, least, high):
    def one(axis_at, blocks):
        steps = jax.random.uniform(jax.random.fold_in(jax.random.fold_in(own_key, 6), axis_at), (blocks,), jnp.float32, least / len(split), high / len(split))
        return jnp.repeat(jnp.exp(steps), dims[axis_at] // blocks).reshape((-1,) + (1,) * (len(dims) - axis_at - 1))

    level = one(*split[0])
    for cut in split[1:]:
        level = level * one(*cut)
    return level


def scatter_about(stream_key, extent, scale, limit, pieces=(), held_as=jnp.bfloat16):
    array = jax.random.normal(stream_key, extent, jnp.float32) * scale
    if len(pieces) > 0:
        array = block_scale(stream_key, extent, pieces, -0.22, 0.18) * array
    return jnp.clip(array, min=-limit, max=limit).astype(held_as)


def setup_inputs(seed: int = 0) -> dict:
    keys = jax.random.split(jax.random.key(seed), 13)
    return {
        "q_row": draw_q_row(jax.random.fold_in(keys[12], 71), 0),
        "k_row": draw_k_row(jax.random.fold_in(keys[12], 71), 0),
        "v_row": scatter_about(keys[2], (BATCH, G, G, D), 1.0, 6.0, ((0, 4), (1, 8))),
        "q_col": draw_q_col(jax.random.fold_in(keys[12], 71), 0),
        "k_col": draw_k_col(jax.random.fold_in(keys[12], 71), 0),
        "cotangent": scatter_about(keys[5], (BATCH, G, G, D), 1.0, 6.0, ((0, 4), (2, 8))),
        "w_value": scatter_about(keys[6], (D, D), D ** -0.5, 0.15625, ((0, 32),)),
        "row_positions": jax.random.permutation(keys[7], G).astype(jnp.int32),
        "col_positions": jax.random.permutation(keys[8], G).astype(jnp.int32),
        "mlp_in": scatter_about(keys[9], (HM,), 2.0, 8.0, ((0, 8),), jnp.float32),
        "mlp_bias": scatter_about(keys[10], (HM,), 1.0, 4.0, ((0, 8),), jnp.float32),
        "mlp_out": scatter_about(keys[11], (HM, NH), 0.013, 0.08, ((0, 8),), jnp.float32),
    }


PRECISE = lax.Precision.HIGHEST

def offset_coords():
    delta = jnp.arange(NOFF, dtype=jnp.float32) - (G - 1)
    scaled = delta * (8.0 / (G - 1))
    return jnp.sign(scaled) * jnp.log2(jnp.abs(scaled) + 1.0) / 3.0

def offset_one_hot(positions):
    spread = positions[:, None].astype(jnp.int32) - positions[None, :].astype(jnp.int32) + (G - 1)
    levels = jnp.arange(NOFF, dtype=jnp.int32)
    return (spread.reshape(-1)[:, None] == levels[None, :]).astype(jnp.float32)

def expand_bias(one_hot, bias_table):
    flat_bias = jnp.dot(one_hot, bias_table, precision=PRECISE)
    return flat_bias.reshape(G, G, NH).transpose(2, 0, 1)

def fold_bias(one_hot, bias_grad):
    flat_grad = bias_grad.transpose(1, 2, 0).reshape(G * G, NH)
    return lax.dot_general(one_hot, flat_grad, (((0,), (0,)), ((), ())), precision=PRECISE)

def soft_grad(attn_probs, d_probs):
    return attn_probs * (d_probs - lax.optimization_barrier(jnp.sum(attn_probs * d_probs, axis=-1, keepdims=True)))

def widen(narrow):
    return lax.optimization_barrier(narrow).astype(jnp.float32)

def reference(q_row, k_row, v_row, q_col, k_col, cotangent, w_value, row_positions, col_positions, mlp_in, mlp_bias, mlp_out):
    coords = offset_coords()
    pre_act = coords[:, None] * mlp_in[None, :] + mlp_bias[None, :]
    hidden_units = jnp.maximum(pre_act, 0.0)
    table_pre = jnp.dot(hidden_units, mlp_out, precision=PRECISE)
    squashed = jax.nn.sigmoid(table_pre)
    bias_table = 16.0 * squashed
    hot_cols = offset_one_hot(col_positions)
    hot_rows = offset_one_hot(row_positions)
    bias_row = expand_bias(hot_cols, bias_table)
    bias_col = expand_bias(hot_rows, bias_table)
    score_scale = HD ** (-0.5)

    def one_image(carry, items):
        row_query, row_key, row_value, col_query, col_key, grad_out = items
        query_rows = row_query.astype(jnp.float32).reshape(G, G, NH, HD)
        key_rows = row_key.astype(jnp.float32).reshape(G, G, NH, HD)
        value_rows = row_value.astype(jnp.float32).reshape(G, G, NH, HD)
        scores = jnp.einsum('nqhd,nkhd->nhqk', query_rows, key_rows) * score_scale + bias_row[None]
        p_row = jax.nn.softmax(scores, axis=-1)
        p_row_b = p_row.astype(jnp.bfloat16)
        row_out = jnp.einsum('nhqk,nkhd->nqhd', widen(p_row_b), value_rows).astype(jnp.bfloat16)
        projected = jnp.dot(row_out.reshape(G * G, D), w_value, preferred_element_type=jnp.float32)
        col_values = projected.astype(jnp.bfloat16)
        value_cols = widen(col_values).reshape(G, G, NH, HD)
        query_cols = col_query.astype(jnp.float32).reshape(G, G, NH, HD)
        key_cols = col_key.astype(jnp.float32).reshape(G, G, NH, HD)
        scores_col = jnp.einsum('qchd,kchd->chqk', query_cols, key_cols) * score_scale + bias_col[None]
        p_col = jax.nn.softmax(scores_col, axis=-1)
        p_col_w = widen(p_col.astype(jnp.bfloat16))
        attended = jnp.einsum('chqk,kchd->qchd', p_col_w, value_cols).astype(jnp.bfloat16).reshape(G, G, D)
        grad_cols = grad_out.astype(jnp.float32).reshape(G, G, NH, HD)
        dprob_col = jnp.einsum('qchd,kchd->chqk', grad_cols, value_cols)
        ds_col = soft_grad(p_col, dprob_col)
        d_values = jnp.einsum('chqk,qchd->kchd', p_col_w, grad_cols).astype(jnp.bfloat16).reshape(G * G, D)
        d_flat = lax.dot_general(d_values, w_value, (((1,), (1,)), ((), ())), preferred_element_type=jnp.float32)
        d_row_out = widen(d_flat.astype(jnp.bfloat16)).reshape(G, G, NH, HD)
        dprob_row = jnp.einsum('nqhd,nkhd->nhqk', d_row_out, value_rows)
        ds_row = soft_grad(p_row, dprob_row)
        return ((carry[0] + lax.optimization_barrier(jnp.sum(ds_row, axis=0)), carry[1] + lax.optimization_barrier(jnp.sum(ds_col, axis=0))), attended)
    start = (jnp.zeros((NH, G, G), jnp.float32), jnp.zeros((NH, G, G), jnp.float32))
    sums, attended = lax.scan(one_image, start, (q_row, k_row, v_row, q_col, k_col, cotangent))
    row_table = fold_bias(hot_cols, sums[0])
    col_table = fold_bias(hot_rows, sums[1])
    table_grad = (row_table + col_table) / (BATCH * G)
    pre_grad = table_grad * 16.0 * squashed * (1.0 - squashed)
    grad_mlp_out = lax.dot_general(hidden_units, pre_grad, (((0,), (0,)), ((), ())), precision=PRECISE)
    back_units = lax.dot_general(pre_grad, mlp_out, (((1,), (1,)), ((), ())), precision=PRECISE)
    unit_grad = jnp.where(pre_act > 0, back_units, 0.0)
    grad_mlp_in = lax.optimization_barrier(jnp.sum(unit_grad * coords[:, None], axis=0))
    grad_mlp_bias = lax.optimization_barrier(jnp.sum(unit_grad, axis=0))
    return (attended, grad_mlp_in, grad_mlp_bias, grad_mlp_out)
```

```python
import functools
import math

import jax
import jax.numpy as jnp
from jax import lax
from jax.experimental import pallas as pl
from jax.experimental.pallas import tpu as pltpu
from jax.sharding import PartitionSpec as P

LANES = 128
F32 = jnp.float32
BF16 = jnp.bfloat16
PRECISE = lax.Precision.HIGHEST


def offset_coords(tokens):
    delta = jnp.arange(2 * tokens - 1, dtype=F32) - (tokens - 1)
    scaled = delta * (8.0 / (tokens - 1))
    return jnp.sign(scaled) * jnp.log2(jnp.abs(scaled) + 1.0) / 3.0


def offset_one_hot(positions, tokens):
    spread = positions[None, :] - positions[:, None] + (tokens - 1)
    levels = jnp.arange(2 * tokens - 1, dtype=jnp.int32)
    return (levels[:, None] == spread.reshape(-1)[None, :]).astype(F32)


def spread_sum(x, axis_name):
    n = lax.axis_size(axis_name)
    copies = jnp.broadcast_to(x[None], (n,) + x.shape)
    return jnp.sum(lax.all_to_all(copies, axis_name, 0, 0), axis=0)


def stacked(x, hd):
    lane = lax.broadcasted_iota(jnp.int32, (1, LANES), 1) // hd
    return jnp.concatenate(
        [x * (lane == h).astype(F32).astype(BF16) for h in range(LANES // hd)], axis=0
    )


def dot(a, b, ca, cb):
    return lax.dot_general(a, b, (((ca,), (cb,)), ((), ())), preferred_element_type=F32)


def probs(k, q_stack, bias, scale):
    s = dot(k, q_stack, 1, 1) * scale + bias
    e = jnp.exp2(s - jnp.max(s, axis=0, keepdims=True))
    return e * (1.0 / jnp.sum(e, axis=0, keepdims=True))


def mix(p, v, hd):
    tokens = v.shape[0]
    full = dot(v, p, 0, 0)
    parts = [
        full[h * hd : (h + 1) * hd, h * tokens : (h + 1) * tokens] for h in range(LANES // hd)
    ]
    return jnp.concatenate(parts, axis=0).T


def soft_grad(p, dp):
    return p * (dp - jnp.sum(p * dp, axis=0, keepdims=True))


def load_bias(bias_ref, bias_s, heads):
    @pl.when(pl.program_id(1) == 0)
    def _():
        bias_s[...] = jnp.concatenate(
            [bias_ref[h] * math.log2(math.e) for h in range(heads)], axis=1
        )


def unpack_columns(ref, scratch, stride):
    tokens, columns = ref.shape[1], ref.shape[2]
    wide = scratch.reshape(tokens, stride, LANES)
    wide[:, 0:columns, :] = ref[0].astype(F32)


def column(scratch, j, tokens, stride):
    return scratch[pl.ds(j, tokens, stride=stride), :]


def pack_columns(ref, scratch, stride):
    tokens, columns = ref.shape[1], ref.shape[2]
    wide = scratch.reshape(tokens, stride, LANES)
    ref[0] = wide[:, 0:columns, :].astype(BF16)


def row_forward(hd, q_ref, k_ref, v_ref, bias_ref, out_ref, p_ref, bias_s):
    load_bias(bias_ref, bias_s, LANES // hd)
    scale = hd**-0.5 * math.log2(math.e)
    for r in range(q_ref.shape[1]):
        p = probs(k_ref[0, r], stacked(q_ref[0, r], hd), bias_s[...], scale).astype(BF16)
        p_ref[0, r, 0] = p
        out_ref[0, r] = mix(p, v_ref[0, r], hd).astype(BF16)


def fold_out(acc, ds_ref, heads):
    @pl.when(pl.program_id(1) == pl.num_programs(1) - 1)
    def _():
        tokens = ds_ref.shape[1]
        for h in range(heads):
            ds_ref[h] = acc[:, h * tokens : (h + 1) * tokens]


def start_acc(acc):
    @pl.when(pl.program_id(1) == 0)
    def _():
        acc[...] = jnp.zeros_like(acc)


def row_backward(hd, p_ref, v_ref, d_ref, ds_ref, acc):
    start_acc(acc)
    for r in range(v_ref.shape[1]):
        dp = dot(v_ref[0, r], stacked(d_ref[0, r], hd), 1, 1)
        acc[...] += soft_grad(p_ref[0, r, 0].astype(F32), dp)
    fold_out(acc, ds_ref, LANES // hd)


def col_forward(hd, stride, q_ref, k_ref, c_ref, bias_ref, dv_ref, p_ref, bias_s, qs, ks, cs, os):
    load_bias(bias_ref, bias_s, LANES // hd)
    scale = hd**-0.5 * math.log2(math.e)
    tokens, columns = q_ref.shape[1], q_ref.shape[2]
    for ref, scratch in ((q_ref, qs), (k_ref, ks), (c_ref, cs)):
        unpack_columns(ref, scratch, stride)
    for j in range(columns):
        q, k, c = (column(s, j, tokens, stride).astype(BF16) for s in (qs, ks, cs))
        p = probs(k, stacked(q, hd), bias_s[...], scale).astype(BF16)
        p_ref[0, j, 0] = p
        os[pl.ds(j, tokens, stride=stride), :] = dot(p, stacked(c, hd), 1, 0)
    pack_columns(dv_ref, os, stride)


def col_backward(hd, stride, p_ref, v_ref, c_ref, out_ref, ds_ref, acc, vs, cs, os):
    start_acc(acc)
    tokens, columns = v_ref.shape[1], v_ref.shape[2]
    for ref, scratch in ((v_ref, vs), (c_ref, cs)):
        unpack_columns(ref, scratch, stride)
    for j in range(columns):
        v, c = (column(s, j, tokens, stride).astype(BF16) for s in (vs, cs))
        p = p_ref[0, j, 0]
        os[pl.ds(j, tokens, stride=stride), :] = mix(p, v, hd)
        dp = dot(v, stacked(c, hd), 1, 1)
        acc[...] += soft_grad(p.astype(F32), dp)
    pack_columns(out_ref, os, stride)
    fold_out(acc, ds_ref, LANES // hd)


def shards(
    q_row,
    k_row,
    v_row,
    q_col,
    k_col,
    cotangent,
    w_value,
    row_positions,
    col_positions,
    mlp_in,
    mlp_bias,
    mlp_out,
):
    images, row_count, tokens, width = q_row.shape
    col_count = q_col.shape[2]
    n_heads = mlp_out.shape[1]
    hd = width // n_heads
    heads = LANES // hd
    chunks = width // LANES
    wide = heads * tokens
    stride = -(-col_count // 8) * 8
    n_off = 2 * tokens - 1

    whole_weight = lax.all_gather(w_value, ("dp", "grid"), axis=0, tiled=True)

    coords = offset_coords(tokens)
    pre_act = coords[:, None] * mlp_in[None, :] + mlp_bias[None, :]
    hidden_units = jnp.maximum(pre_act, 0.0)
    partial_table = lax.dot_general(
        mlp_out, hidden_units, (((0,), (1,)), ((), ())), precision=PRECISE
    )
    squashed = jax.nn.sigmoid(spread_sum(partial_table, "grid"))
    bias_table = 16.0 * squashed
    hot_cols = offset_one_hot(col_positions, tokens)
    hot_rows = offset_one_hot(row_positions, tokens)
    bias_row = jnp.dot(bias_table, hot_cols, precision=PRECISE).reshape(n_heads, tokens, tokens)
    bias_col = jnp.dot(bias_table, hot_rows, precision=PRECISE).reshape(n_heads, tokens, tokens)

    row_block = pl.BlockSpec((1, row_count, tokens, LANES), lambda c, n: (n, 0, 0, c))
    col_block = pl.BlockSpec((1, tokens, col_count, LANES), lambda c, n: (n, 0, 0, c))
    head_block = pl.BlockSpec((heads, tokens, tokens), lambda c, n: (c, 0, 0))
    row_p_block = pl.BlockSpec((1, row_count, 1, tokens, wide), lambda c, n: (n, 0, c, 0, 0))
    col_p_block = pl.BlockSpec((1, col_count, 1, tokens, wide), lambda c, n: (n, 0, c, 0, 0))
    row_shape = jax.ShapeDtypeStruct((images, row_count, tokens, width), BF16)
    col_shape = jax.ShapeDtypeStruct((images, tokens, col_count, width), BF16)
    row_p_shape = jax.ShapeDtypeStruct((images, row_count, chunks, tokens, wide), BF16)
    col_p_shape = jax.ShapeDtypeStruct((images, col_count, chunks, tokens, wide), BF16)
    sums_shape = jax.ShapeDtypeStruct((n_heads, tokens, tokens), F32)
    square = pltpu.VMEM((tokens, wide), F32)
    column_scratch = pltpu.VMEM((tokens * stride, LANES), F32)
    grid = (chunks, images)
    params = pltpu.CompilerParams(vmem_limit_bytes=56 * 1024 * 1024)
    cost = pl.CostEstimate(
        flops=40 * 2**30, bytes_accessed=60 * 2**20, transcendentals=20 * 2**20
    )

    def call(body, in_specs, out_specs, out_shape, scratch, name):
        return pl.pallas_call(
            body,
            grid=grid,
            in_specs=in_specs,
            out_specs=out_specs,
            out_shape=out_shape,
            scratch_shapes=scratch,
            compiler_params=params,
            cost_estimate=cost,
            name=name,
        )

    d_values, p_col = call(
        functools.partial(col_forward, hd, stride),
        [col_block, col_block, col_block, head_block],
        [col_block, col_p_block],
        [col_shape, col_p_shape],
        [square] + [column_scratch] * 4,
        "col_forward",
    )(q_col, k_col, cotangent, bias_col)
    d_rows = lax.all_to_all(d_values, "grid", split_axis=1, concat_axis=2, tiled=True)

    row_out, p_row = call(
        functools.partial(row_forward, hd),
        [row_block, row_block, row_block, head_block],
        [row_block, row_p_block],
        [row_shape, row_p_shape],
        [square],
        "row_forward",
    )(q_row, k_row, v_row, bias_row)
    flat_out = row_out.reshape(images * row_count * tokens, width)
    values = jnp.dot(flat_out, whole_weight, preferred_element_type=F32).astype(BF16)
    values = values.reshape(images, row_count, tokens, width)
    col_values = lax.all_to_all(values, "grid", split_axis=2, concat_axis=1, tiled=True)

    flat_grad = d_rows.reshape(images * row_count * tokens, width)
    d_row_out = dot(flat_grad, whole_weight, 1, 1).astype(BF16)
    d_row_out = d_row_out.reshape(images, row_count, tokens, width)
    row_sums = call(
        functools.partial(row_backward, hd),
        [row_p_block, row_block, row_block],
        head_block,
        sums_shape,
        [square],
        "row_backward",
    )(p_row, v_row, d_row_out)

    attended, col_sums = call(
        functools.partial(col_backward, hd, stride),
        [col_p_block, col_block, col_block],
        [col_block, head_block],
        [col_shape, sums_shape],
        [square] + [column_scratch] * 3,
        "col_backward",
    )(p_col, col_values, cotangent)

    def fold(sums, hot):
        flat = sums.reshape(n_heads, tokens * tokens)
        return lax.dot_general(flat, hot, (((1,), (1,)), ((), ())), precision=PRECISE)

    table = fold(row_sums, hot_cols) + fold(col_sums, hot_rows)
    table_sum = spread_sum(spread_sum(table, "grid"), "dp")
    batch_size = lax.axis_size("dp") * images
    table_grad = table_sum / (batch_size * tokens)
    pre_grad = table_grad * 16.0 * squashed * (1.0 - squashed)
    grad_mlp_out = lax.dot_general(
        hidden_units, pre_grad, (((0,), (1,)), ((), ())), precision=PRECISE
    )
    back_units = lax.dot_general(pre_grad, mlp_out, (((0,), (1,)), ((), ())), precision=PRECISE)
    unit_grad = jnp.where(pre_act > 0, back_units, 0.0)
    grad_mlp_in = jnp.sum(unit_grad * coords[:, None], axis=0)
    grad_mlp_bias = jnp.sum(unit_grad, axis=0)
    return (attended, grad_mlp_in, grad_mlp_bias, grad_mlp_out)


def solution(mesh):
    return jax.shard_map(
        shards,
        mesh=mesh,
        in_specs=(
            P("dp", "grid", None, None),
            P("dp", "grid", None, None),
            P("dp", "grid", None, None),
            P("dp", None, "grid", None),
            P("dp", None, "grid", None),
            P("dp", None, "grid", None),
            P(("dp", "grid"), None),
            P(),
            P(),
            P("grid"),
            P("grid"),
            P("grid", None),
        ),
        out_specs=(P("dp", None, "grid", None), P("grid"), P("grid"), P("grid", None)),
        check_vma=False,
    )
```
